32 devices in a mesh: rows: 8 (over z, y), layers: 4 (over x, core).
Axes of the slice: x: 2, y: 2, z: 4, core: 2. Of those that a mesh axis runs over, the one named last changes fastest.
Arguments:
- queries: bfloat16 [256, 4, 4096], P('rows', 'layers'), may hold values from -6 to 6
- precond: bfloat16 [4, 4096, 4096], P('layers', None, 'rows'), as said below
- train_grads: bfloat16 [16384, 4, 4096], P('rows', 'layers'), may hold values from -0.09375 to 0.09375
Outputs:
- scores: float32 [256, 16384], P('layers', 'rows')
The draws below stay inside these ranges and needn't reach their ends.
Inputs may be any that keep to these rules, and one draw needn't show every extreme that they name: `precond`: symmetric in its last two dimensions.
All inputs are finite; a program needn't handle non-finite values.
Results may differ from the reference program's by a relative error of at most 0.0029.
Values may be sent and summed in bfloat16 or wider, within the bound.
A program may use at most 128 MiB of HBM per device.

```python
import jax
import jax.numpy as jnp

F = 4096
LAYERS = 4
NQ = 256
NT = 16384


def draw_precond(key, part):
    key_off = jax.random.fold_in(key, 11)
    key_diag = jax.random.fold_in(key, 12)
    noise = jax.random.normal(key_off, (LAYERS, F, F), jnp.float32) * (0.5 / F ** 0.5)
    sym = noise + jnp.swapaxes(noise, 1, 2)
    diag_vals = jax.random.uniform(key_diag, (LAYERS, F), jnp.float32, 0.5, 2.0)
    eye_mask = (jnp.arange(F)[:, None] == jnp.arange(F)[None, :]).astype(jnp.float32)
    matrix = sym + eye_mask[None, :, :] * diag_vals[:, :, None]
    return matrix.astype(jnp.bfloat16)


def levels(key, dims, shards, least, top_value):
    def one(position, blocks):
        draws = jax.random.uniform(jax.random.fold_in(jax.random.fold_in(key, 6), position), (blocks,), jnp.float32, least / len(shards), top_value / len(shards))
        return jnp.repeat(jnp.exp(draws), dims[position] // blocks).reshape((-1,) + (1,) * (len(dims) - position - 1))

    level = one(*shards[0])
    for cut in shards[1:]:
        level = level * one(*cut)
    return level


def bell_draw(stream_key, extent, width, reach, split=(), kind=jnp.bfloat16):
    gain = levels(stream_key, extent, split, -0.22, 0.18) if split else 1.0
    array = jax.random.normal(stream_key, extent, jnp.float32) * width * gain
    return jnp.minimum(jnp.maximum(array, -reach), reach).astype(kind)


def setup_inputs(seed: int = 0) -> dict:
    key_of = jax.random.split(jax.random.key(seed), 4)
    queries = bell_draw(key_of[0], (NQ, LAYERS, F), 1.0, 6.0, ((0, 8), (1, 4)))
    precond = draw_precond(jax.random.fold_in(key_of[3], 71), 0)
    train_grads = bell_draw(key_of[2], (NT, LAYERS, F), F ** -0.5, 0.09375, ((0, 8), (1, 4)))
    return {"queries": queries, "precond": precond, "train_grads": train_grads}


def reference(queries, precond, train_grads):
    scores = jnp.zeros((NQ, NT), jnp.float32)
    for layer in range(LAYERS):
        conditioned = jnp.dot(queries[:, layer, :], precond[layer], preferred_element_type=jnp.float32).astype(jnp.bfloat16)
        scores = scores + jnp.dot(conditioned, train_grads[:, layer, :].T, preferred_element_type=jnp.float32)
    return scores
```

```python
import functools

import jax
import jax.numpy as jnp
from jax import lax
from jax.experimental import pallas as pl
from jax.experimental.pallas import tpu as pltpu
from jax.sharding import PartitionSpec as P

MESH = pl.DeviceIdType.MESH
RIGHT, LEFT, ACROSS = 0, 1, 2


def kernel(
    line, q_hbm, p_hbm, t_hbm, out_ref,
    qbuf, cbuf, pv, tv, cacc, acc, crecv, xsend, xrecv,
    local_sem, send_sem, recv_sem, csend_sem, crecv_sem, xsend_sem, xrecv_sem,
):
    row, layer = lax.axis_index("rows"), lax.axis_index("layers")
    k, y = row // 2, row % 2
    x, core = layer // 2, layer % 2
    units, half_rows = qbuf.shape[1], qbuf.shape[2]
    width = cbuf.shape[3]
    nq = units * half_rows
    features, nt = tv.shape[1], tv.shape[0]
    has_right, has_left = k + 1 < line, k > 0

    def at_row(r):
        return {"rows": r, "layers": layer}

    def at_layer(l):
        return {"rows": row, "layers": l}

    right, left, across = at_row(row + 2), at_row(row - 2), at_row(2 * k + 1 - y)
    core_mate = at_layer(2 * x + 1 - core)
    x_mate = at_layer(2 * (1 - x) + core)

    load_q = [
        pltpu.make_async_copy(q_hbm.at[h], qbuf.at[h, row], local_sem.at[h])
        for h in range(2)
    ]
    load_p = pltpu.make_async_copy(p_hbm, pv, local_sem.at[2])
    load_t = pltpu.make_async_copy(t_hbm, tv, local_sem.at[3])
    load_q[0].start()
    load_q[1].start()
    load_p.start()

    barrier = pltpu.get_barrier_semaphore()
    for mate in (across, core_mate, x_mate):
        pl.semaphore_signal(barrier, inc=1, device_id=mate, device_id_type=MESH)

    @pl.when(has_right)
    def _():
        pl.semaphore_signal(barrier, inc=1, device_id=right, device_id_type=MESH)

    @pl.when(has_left)
    def _():
        pl.semaphore_signal(barrier, inc=1, device_id=left, device_id_type=MESH)

    neighbours = (k + line - 1) // line + (2 * line - 2 - k) // line
    pl.semaphore_wait(barrier, 3 + neighbours)

    def slot(phase, unit):
        return (qbuf if phase < 2 else cbuf).at[phase % 2, unit]

    def copy(phase, kk, side, target, own=False):
        unit = 2 * kk + y
        src = q_hbm.at[phase] if own and phase < 2 else slot(phase, unit)
        return pltpu.make_async_remote_copy(
            src_ref=src,
            dst_ref=slot(phase, unit),
            send_sem=send_sem.at[phase, side, kk],
            recv_sem=recv_sem.at[phase, unit],
            device_id=target,
            device_id_type=MESH,
        )

    def wait_unit(phase, unit):
        pltpu.make_async_remote_copy(
            src_ref=slot(phase, unit),
            dst_ref=slot(phase, unit),
            send_sem=send_sem.at[phase, ACROSS, 0],
            recv_sem=recv_sem.at[phase, unit],
            device_id=across,
            device_id_type=MESH,
        ).wait_recv()

    def open_phase(phase):
        @pl.when(has_right)
        def _():
            copy(phase, k, RIGHT, right, own=True).start()

        @pl.when(has_left)
        def _():
            copy(phase, k, LEFT, left, own=True).start()

        copy(phase, k, ACROSS, across, own=True).start()

    def forward(phase, s):
        @pl.when(k - s >= 0)
        def _():
            wait_unit(phase, 2 * (k - s) + y)

            @pl.when(has_right)
            def _():
                copy(phase, k - s, RIGHT, right).start()

            copy(phase, k - s, ACROSS, across).start()

        @pl.when(k + s < line)
        def _():
            wait_unit(phase, 2 * (k + s) + y)

            @pl.when(has_left)
            def _():
                copy(phase, k + s, LEFT, left).start()

            copy(phase, k + s, ACROSS, across).start()

    def forward_all(phase):
        lax.fori_loop(1, line, lambda s, c: (forward(phase, s), c)[1], 0)

    def wait_across(phase):
        lax.fori_loop(
            0, line, lambda kk, c: (wait_unit(phase, 2 * kk + 1 - y), c)[1], 0
        )

    depth = min(512, features)

    def condition(h):
        cacc[...] = jnp.zeros_like(cacc)

        def body(i, c):
            cut = pl.ds(pl.multiple_of(i * depth, depth), depth)
            cacc[...] += jnp.dot(
                qbuf[h, :, :, cut].reshape(nq, depth), pv[cut, :],
                preferred_element_type=jnp.float32,
            )
            return c

        lax.fori_loop(0, features // depth, body, 0)
        cbuf[h, row] = cacc[...].astype(jnp.bfloat16)

    tile = min(512, nt)

    def score(h, unit):
        cols = pl.ds(pl.multiple_of(unit * width, width), width)

        def body(i, c):
            rows = pl.ds(pl.multiple_of(i * tile, tile), tile)
            part = lax.dot_general(
                cbuf[h, unit], tv[rows, cols], (((1,), (1,)), ((), ())),
                preferred_element_type=jnp.float32,
            )
            acc[h, :, :, rows] += part.reshape(4, nq // 4, tile)
            return c

        lax.fori_loop(0, nt // tile, body, 0)

    def score_step(h, s):
        def both(kk):
            score(h, 2 * kk + y)
            wait_unit(2 + h, 2 * kk + 1 - y)
            score(h, 2 * kk + 1 - y)

        pl.when(k - s >= 0)(lambda: both(k - s))
        pl.when((s > 0) & (k + s < line))(lambda: both(k + s))

    def core_copy(h, xx):
        return pltpu.make_async_remote_copy(
            src_ref=acc.at[h, 2 * xx + 1 - core],
            dst_ref=crecv.at[h, xx],
            send_sem=csend_sem.at[h, xx],
            recv_sem=crecv_sem.at[h, xx],
            device_id=core_mate,
            device_id_type=MESH,
        )

    def x_copy(h):
        return pltpu.make_async_remote_copy(
            src_ref=xsend.at[h],
            dst_ref=xrecv.at[h],
            send_sem=xsend_sem.at[h],
            recv_sem=xrecv_sem.at[h],
            device_id=x_mate,
            device_id_type=MESH,
        )

    def reduce_open(h):
        core_copy(h, 1 - x).start()
        core_copy(h, x).start()

    def reduce_core(h):
        core_copy(h, 1 - x).wait_recv()
        xsend[h] = (acc[h, 2 * (1 - x) + core] + crecv[h, 1 - x]).astype(jnp.bfloat16)
        x_copy(h).start()

    def reduce_close(h):
        core_copy(h, x).wait_recv()
        x_copy(h).wait_recv()
        total = acc[h, layer] + crecv[h, x] + xrecv[h].astype(jnp.float32)
        out_ref[:, h] = total.reshape(out_ref.shape[0], half_rows, nt)

    open_phase(0)
    load_t.start()
    acc[...] = jnp.zeros_like(acc)
    forward_all(0)
    open_phase(1)
    load_q[0].wait()
    load_p.wait()
    wait_across(0)
    condition(0)
    forward_all(1)
    open_phase(2)
    load_q[1].wait()
    wait_across(1)
    condition(1)
    load_t.wait()

    def first(s, c):
        forward(2, s)
        score_step(0, s - 1)
        return c

    lax.fori_loop(1, line, first, 0)
    open_phase(3)
    score_step(0, line - 1)
    reduce_open(0)

    def second(s, c):
        forward(3, s)
        pl.when(s == 1)(lambda: reduce_core(0))
        score_step(1, s - 1)
        return c

    lax.fori_loop(1, line, second, 0)
    reduce_close(0)
    score_step(1, line - 1)
    reduce_open(1)
    reduce_core(1)
    reduce_close(1)

    for phase in range(4):

        def drain(kk, c):
            pl.when(has_right & (kk <= k))(
                lambda: copy(phase, kk, RIGHT, right).wait_send()
            )
            pl.when(has_left & (kk >= k))(
                lambda: copy(phase, kk, LEFT, left).wait_send()
            )
            copy(phase, kk, ACROSS, across).wait_send()
            return c

        lax.fori_loop(0, line, drain, 0)
    for h in range(2):
        core_copy(h, x).wait_send()
        core_copy(h, 1 - x).wait_send()
        x_copy(h).wait_send()


def per_device(units, queries, precond, train_grads):
    own, _, features = queries.shape
    width = precond.shape[2]
    nt = train_grads.shape[0]
    half_rows = own // 2
    nq = units * half_rows
    line = units // 2
    bf16, f32 = jnp.bfloat16, jnp.float32
    anywhere = pl.BlockSpec(memory_space=pl.ANY)
    flops = 2 * 2 * nq * features * (width + nt)
    out = pl.pallas_call(
        functools.partial(kernel, line),
        out_shape=jax.ShapeDtypeStruct((units // 4, 2, half_rows, nt), f32),
        in_specs=[anywhere] * 3,
        out_specs=pl.BlockSpec(memory_space=pltpu.VMEM),
        scratch_shapes=[
            pltpu.VMEM((2, units, half_rows, features), bf16),
            pltpu.VMEM((2, units, nq, width), bf16),
            pltpu.VMEM((features, width), bf16),
            pltpu.VMEM((nt, features), bf16),
            pltpu.VMEM((nq, width), f32),
            pltpu.VMEM((2, 4, nq // 4, nt), f32),
            pltpu.VMEM((2, 2, nq // 4, nt), f32),
            pltpu.VMEM((2, nq // 4, nt), bf16),
            pltpu.VMEM((2, nq // 4, nt), bf16),
            pltpu.SemaphoreType.DMA((4,)),
            pltpu.SemaphoreType.DMA((4, 3, line)),
            pltpu.SemaphoreType.DMA((4, units)),
            pltpu.SemaphoreType.DMA((2, 2)),
            pltpu.SemaphoreType.DMA((2, 2)),
            pltpu.SemaphoreType.DMA((2,)),
            pltpu.SemaphoreType.DMA((2,)),
        ],
        compiler_params=pltpu.CompilerParams(
            collective_id=0, has_side_effects=True, vmem_limit_bytes=60 << 20
        ),
        cost_estimate=pl.CostEstimate(
            flops=flops, bytes_accessed=2 * features * (width + nt), transcendentals=0
        ),
    )(
        queries.reshape(2, half_rows, features),
        precond.reshape(features, width),
        train_grads.reshape(nt, features),
    )
    return out.reshape(2 * units // 4 * half_rows, nt)


def solution(mesh):
    return jax.shard_map(
        functools.partial(per_device, mesh.shape["rows"]),
        mesh=mesh,
        in_specs=(P("rows", "layers", None), P("layers", None, "rows"), P("rows", "layers", None)),
        out_specs=P("layers", "rows"),
        check_vma=False,
    )
```

```python
import functools

import jax
import jax.numpy as jnp
from jax import lax
from jax.experimental import pallas as pl
from jax.experimental.pallas import tpu as pltpu
from jax.sharding import PartitionSpec as P

MESH = pl.DeviceIdType.MESH
ALONG, ACROSS = 0, 1


def kernel(
    line, q_hbm, p_hbm, t_hbm, out_ref,
    qbuf, cbuf, pv, tv, cacc, acc, crecv, xsend, xrecv,
    local_sem, send_sem, recv_sem, csend_sem, crecv_sem, xsend_sem, xrecv_sem,
):
    row, layer = lax.axis_index("rows"), lax.axis_index("layers")
    k, y = row // 2, row % 2
    x, core = layer // 2, layer % 2
    units, half_rows = qbuf.shape[1], qbuf.shape[2]
    width = cbuf.shape[3]
    nq = units * half_rows
    features, nt = tv.shape[1], tv.shape[0]

    def at_row(r):
        return {"rows": r, "layers": layer}

    def at_layer(l):
        return {"rows": row, "layers": l}

    across = at_row(2 * k + 1 - y)
    core_mate = at_layer(2 * x + 1 - core)
    x_mate = at_layer(2 * (1 - x) + core)

    load_q = [
        pltpu.make_async_copy(q_hbm.at[h], qbuf.at[h, row], local_sem.at[h])
        for h in range(2)
    ]
    load_p = pltpu.make_async_copy(p_hbm, pv, local_sem.at[2])
    load_t = pltpu.make_async_copy(t_hbm, tv, local_sem.at[3])
    load_q[0].start()
    load_q[1].start()
    load_p.start()

    barrier = pltpu.get_barrier_semaphore()
    for mate in (across, core_mate, x_mate):
        pl.semaphore_signal(barrier, inc=1, device_id=mate, device_id_type=MESH)

    def each_on_line(act):
        def body(kk, c):
            pl.when(kk != k)(lambda: act(kk))
            return c

        lax.fori_loop(0, line, body, 0)

    def greet(kk):
        pl.semaphore_signal(
            barrier, inc=1, device_id=at_row(2 * kk + y), device_id_type=MESH
        )

    each_on_line(greet)
    pl.semaphore_wait(barrier, 3 + line - 1)

    def slot(phase, unit):
        return (qbuf if phase < 2 else cbuf).at[phase % 2, unit]

    def along(phase, kk):
        return pltpu.make_async_remote_copy(
            src_ref=q_hbm.at[phase] if phase < 2 else slot(phase, row),
            dst_ref=slot(phase, row),
            send_sem=send_sem.at[phase, ALONG, kk],
            recv_sem=recv_sem.at[phase, row],
            device_id=at_row(2 * kk + y),
            device_id_type=MESH,
        )

    def relay_copy(phase, kk, own=False):
        unit = 2 * kk + y
        return pltpu.make_async_remote_copy(
            src_ref=q_hbm.at[phase] if own and phase < 2 else slot(phase, unit),
            dst_ref=slot(phase, unit),
            send_sem=send_sem.at[phase, ACROSS, kk],
            recv_sem=recv_sem.at[phase, unit],
            device_id=across,
            device_id_type=MESH,
        )

    def wait_unit(phase, unit):
        pltpu.make_async_remote_copy(
            src_ref=slot(phase, unit),
            dst_ref=slot(phase, unit),
            send_sem=send_sem.at[phase, ACROSS, 0],
            recv_sem=recv_sem.at[phase, unit],
            device_id=across,
            device_id_type=MESH,
        ).wait_recv()

    def open_phase(phase):
        relay_copy(phase, k, own=True).start()

        def body(d, c):
            pl.when(k + d < line)(lambda: along(phase, k + d).start())
            pl.when(k - d >= 0)(lambda: along(phase, k - d).start())
            return c

        lax.fori_loop(1, line, body, 0)

    def relay(phase, s):
        def one(kk):
            wait_unit(phase, 2 * kk + y)
            relay_copy(phase, kk).start()

        pl.when(k - s >= 0)(lambda: one(k - s))
        pl.when(k + s < line)(lambda: one(k + s))

    def relay_rest(phase, start):
        lax.fori_loop(start, line, lambda s, c: (relay(phase, s), c)[1], 0)

    def wait_across(phase):
        lax.fori_loop(
            0, line, lambda kk, c: (wait_unit(phase, 2 * kk + 1 - y), c)[1], 0
        )

    depth = min(512, features)

    def condition(h):
        cacc[...] = jnp.zeros_like(cacc)

        def body(i, c):
            cut = pl.ds(pl.multiple_of(i * depth, depth), depth)
            cacc[...] += jnp.dot(
                qbuf[h, :, :, cut].reshape(nq, depth), pv[cut, :],
                preferred_element_type=jnp.float32,
            )
            return c

        lax.fori_loop(0, features // depth, body, 0)
        cbuf[h, row] = cacc[...].astype(jnp.bfloat16)

    tile = min(512, nt)

    def score(h, unit):
        cols = pl.ds(pl.multiple_of(unit * width, width), width)

        def body(i, c):
            rows = pl.ds(pl.multiple_of(i * tile, tile), tile)
            part = lax.dot_general(
                cbuf[h, unit], tv[rows, cols], (((1,), (1,)), ((), ())),
                preferred_element_type=jnp.float32,
            )
            acc[h, :, :, rows] += part.reshape(4, nq // 4, tile)
            return c

        lax.fori_loop(0, nt // tile, body, 0)

    def score_line(h, s):
        pl.when(k - s >= 0)(lambda: score(h, 2 * (k - s) + y))
        pl.when((s > 0) & (k + s < line))(lambda: score(h, 2 * (k + s) + y))

    def score_across(h, s):
        def one(kk):
            wait_unit(2 + h, 2 * kk + 1 - y)
            score(h, 2 * kk + 1 - y)

        pl.when(k - s >= 0)(lambda: one(k - s))
        pl.when((s > 0) & (k + s < line))(lambda: one(k + s))

    def core_copy(h, xx):
        return pltpu.make_async_remote_copy(
            src_ref=acc.at[h, 2 * xx + 1 - core],
            dst_ref=crecv.at[h, xx],
            send_sem=csend_sem.at[h, xx],
            recv_sem=crecv_sem.at[h, xx],
            device_id=core_mate,
            device_id_type=MESH,
        )

    def x_copy(h):
        return pltpu.make_async_remote_copy(
            src_ref=xsend.at[h],
            dst_ref=xrecv.at[h],
            send_sem=xsend_sem.at[h],
            recv_sem=xrecv_sem.at[h],
            device_id=x_mate,
            device_id_type=MESH,
        )

    def reduce_open(h):
        core_copy(h, 1 - x).start()
        core_copy(h, x).start()

    def reduce_core(h):
        core_copy(h, 1 - x).wait_recv()
        xsend[h] = (acc[h, 2 * (1 - x) + core] + crecv[h, 1 - x]).astype(jnp.bfloat16)
        x_copy(h).start()

    def reduce_close(h):
        core_copy(h, x).wait_recv()
        x_copy(h).wait_recv()
        total = acc[h, layer] + crecv[h, x] + xrecv[h].astype(jnp.float32)
        out_ref[:, h] = total.reshape(out_ref.shape[0], half_rows, nt)

    open_phase(0)
    load_t.start()
    acc[...] = jnp.zeros_like(acc)
    relay(0, 1)
    open_phase(1)
    relay_rest(0, 2)
    load_q[0].wait()
    load_p.wait()
    wait_across(0)
    relay(1, 1)
    condition(0)
    open_phase(2)
    relay_rest(1, 2)
    load_q[1].wait()
    wait_across(1)
    relay(2, 1)
    condition(1)
    open_phase(3)
    relay_rest(2, 2)
    load_t.wait()

    def first(s, c):
        score_line(0, s - 1)
        relay(3, s)
        return c

    lax.fori_loop(1, line, first, 0)
    score_line(0, line - 1)
    lax.fori_loop(0, line, lambda s, c: (score_across(0, s), c)[1], 0)
    reduce_open(0)
    lax.fori_loop(0, line, lambda s, c: (score_line(1, s), c)[1], 0)
    reduce_core(0)

    def last(s, c):
        score_across(1, s)
        pl.when(s == line - 2)(lambda: reduce_close(0))
        return c

    lax.fori_loop(0, line, last, 0)
    reduce_open(1)
    reduce_core(1)
    reduce_close(1)

    for phase in range(4):
        each_on_line(lambda kk: along(phase, kk).wait_send())

        def drain(kk, c):
            relay_copy(phase, kk).wait_send()
            return c

        lax.fori_loop(0, line, drain, 0)
    for h in range(2):
        core_copy(h, x).wait_send()
        core_copy(h, 1 - x).wait_send()
        x_copy(h).wait_send()


def per_device(units, queries, precond, train_grads):
    own, _, features = queries.shape
    width = precond.shape[2]
    nt = train_grads.shape[0]
    half_rows = own // 2
    nq = units * half_rows
    line = units // 2
    bf16, f32 = jnp.bfloat16, jnp.float32
    anywhere = pl.BlockSpec(memory_space=pl.ANY)
    flops = 2 * 2 * nq * features * (width + nt)
    out = pl.pallas_call(
        functools.partial(kernel, line),
        out_shape=jax.ShapeDtypeStruct((units // 4, 2, half_rows, nt), f32),
        in_specs=[anywhere] * 3,
        out_specs=pl.BlockSpec(memory_space=pltpu.VMEM),
        scratch_shapes=[
            pltpu.VMEM((2, units, half_rows, features), bf16),
            pltpu.VMEM((2, units, nq, width), bf16),
            pltpu.VMEM((features, width), bf16),
            pltpu.VMEM((nt, features), bf16),
            pltpu.VMEM((nq, width), f32),
            pltpu.VMEM((2, 4, nq // 4, nt), f32),
            pltpu.VMEM((2, 2, nq // 4, nt), f32),
            pltpu.VMEM((2, nq // 4, nt), bf16),
            pltpu.VMEM((2, nq // 4, nt), bf16),
            pltpu.SemaphoreType.DMA((4,)),
            pltpu.SemaphoreType.DMA((4, 2, line)),
            pltpu.SemaphoreType.DMA((4, units)),
            pltpu.SemaphoreType.DMA((2, 2)),
            pltpu.SemaphoreType.DMA((2, 2)),
            pltpu.SemaphoreType.DMA((2,)),
            pltpu.SemaphoreType.DMA((2,)),
        ],
        compiler_params=pltpu.CompilerParams(
            collective_id=0, has_side_effects=True, vmem_limit_bytes=60 << 20
        ),
        cost_estimate=pl.CostEstimate(
            flops=flops, bytes_accessed=2 * features * (width + nt), transcendentals=0
        ),
    )(
        queries.reshape(2, half_rows, features),
        precond.reshape(features, width),
        train_grads.reshape(nt, features),
    )
    return out.reshape(2 * units // 4 * half_rows, nt)


def solution(mesh):
    return jax.shard_map(
        functools.partial(per_device, mesh.shape["rows"]),
        mesh=mesh,
        in_specs=(P("rows", "layers", None), P("layers", None, "rows"), P("rows", "layers", None)),
        out_specs=P("layers", "rows"),
        check_vma=False,
    )
```

```python
import functools

import jax
import jax.numpy as jnp
from jax import lax
from jax.experimental import pallas as pl
from jax.experimental.pallas import tpu as pltpu
from jax.sharding import PartitionSpec as P

MESH = pl.DeviceIdType.MESH
RIGHT, LEFT, ACROSS, TWICE = 0, 1, 2, 3


def kernel(
    line, q_hbm, p_hbm, t_hbm, out_ref,
    qbuf, cbuf, pv, tv, cacc, acc, crecv, xsend, xrecv,
    local_sem, send_sem, recv_sem, csend_sem, crecv_sem, xsend_sem, xrecv_sem,
):
    row, layer = lax.axis_index("rows"), lax.axis_index("layers")
    k, y = row // 2, row % 2
    x, core = layer // 2, layer % 2
    units, half_rows = qbuf.shape[1], qbuf.shape[2]
    width = cbuf.shape[3]
    nq = units * half_rows
    features, nt = tv.shape[1], tv.shape[0]

    def at_row(r):
        return {"rows": r, "layers": layer}

    def at_layer(l):
        return {"rows": row, "layers": l}

    right, left, across = at_row(row + 2), at_row(row - 2), at_row(2 * k + 1 - y)
    has_right, has_left = k + 1 < line, k > 0
    core_mate = at_layer(2 * x + 1 - core)
    x_mate = at_layer(2 * (1 - x) + core)

    load_q = [
        pltpu.make_async_copy(q_hbm.at[h], qbuf.at[h, row], local_sem.at[h])
        for h in range(2)
    ]
    load_p = pltpu.make_async_copy(p_hbm, pv, local_sem.at[2])
    load_t = pltpu.make_async_copy(t_hbm, tv, local_sem.at[3])
    load_q[0].start()
    load_q[1].start()
    load_p.start()

    barrier = pltpu.get_barrier_semaphore()
    for mate in (across, core_mate, x_mate):
        pl.semaphore_signal(barrier, inc=1, device_id=mate, device_id_type=MESH)

    @pl.when(has_right)
    def _():
        pl.semaphore_signal(barrier, inc=1, device_id=right, device_id_type=MESH)

    @pl.when(has_left)
    def _():
        pl.semaphore_signal(barrier, inc=1, device_id=left, device_id_type=MESH)

    neighbours = (k + line - 1) // line + (2 * line - 2 - k) // line
    pl.semaphore_wait(barrier, 3 + neighbours)

    def slot(phase, unit):
        return (qbuf if phase < 2 else cbuf).at[phase % 2, unit]

    def copy(phase, kk, side, target, own=False):
        unit = 2 * kk + (1 - y if side == TWICE else y)
        return pltpu.make_async_remote_copy(
            src_ref=q_hbm.at[phase] if own and phase < 2 else slot(phase, unit),
            dst_ref=slot(phase, unit),
            send_sem=send_sem.at[phase, side, kk],
            recv_sem=recv_sem.at[phase, unit],
            device_id=target,
            device_id_type=MESH,
        )

    def twice(phase):
        return 0 if phase % 2 == 0 else line - 1

    def wait_unit(phase, unit):
        pltpu.make_async_remote_copy(
            src_ref=slot(phase, unit),
            dst_ref=slot(phase, unit),
            send_sem=send_sem.at[phase, ACROSS, 0],
            recv_sem=recv_sem.at[phase, unit],
            device_id=across,
            device_id_type=MESH,
        ).wait_recv()

    def open_phase(phase):
        pl.when(has_right)(lambda: copy(phase, k, RIGHT, right, own=True).start())
        pl.when(has_left)(lambda: copy(phase, k, LEFT, left, own=True).start())
        copy(phase, k, ACROSS, across, own=True).start()

    def forward(phase, s):
        def onward(kk, side, target, more):
            wait_unit(phase, 2 * kk + y)
            pl.when(more)(lambda: copy(phase, kk, side, target).start())
            pl.when(kk != twice(phase))(lambda: copy(phase, kk, ACROSS, across).start())

        pl.when(k - s >= 0)(lambda: onward(k - s, RIGHT, right, has_right))
        pl.when(k + s < line)(lambda: onward(k + s, LEFT, left, has_left))
        kk = twice(phase)
        distance, side, target, more = (
            (k, RIGHT, right, has_right) if kk == 0 else (kk - k, LEFT, left, has_left)
        )

        @pl.when(s == distance + 1)
        def _():
            wait_unit(phase, 2 * kk + 1 - y)
            pl.when(more)(lambda: copy(phase, kk, TWICE, target).start())

    def wait_across(phase):
        def body(kk, c):
            pl.when(kk != twice(phase))(lambda: wait_unit(phase, 2 * kk + 1 - y))
            return c

        lax.fori_loop(0, line, body, 0)

    def forward_rest(phase, start):
        lax.fori_loop(start, line + 1, lambda s, c: (forward(phase, s), c)[1], 0)

    depth = min(512, features)

    def condition(h):
        cacc[...] = jnp.zeros_like(cacc)

        def body(i, c):
            cut = pl.ds(pl.multiple_of(i * depth, depth), depth)
            cacc[...] += jnp.dot(
                qbuf[h, :, :, cut].reshape(nq, depth), pv[cut, :],
                preferred_element_type=jnp.float32,
            )
            return c

        lax.fori_loop(0, features // depth, body, 0)
        cbuf[h, row] = cacc[...].astype(jnp.bfloat16)

    tile = min(512, nt)

    def score(h, unit):
        cols = pl.ds(pl.multiple_of(unit * width, width), width)

        def body(i, c):
            rows = pl.ds(pl.multiple_of(i * tile, tile), tile)
            part = lax.dot_general(
                cbuf[h, unit], tv[rows, cols], (((1,), (1,)), ((), ())),
                preferred_element_type=jnp.float32,
            )
            acc[h, :, :, rows] += part.reshape(4, nq // 4, tile)
            return c

        lax.fori_loop(0, nt // tile, body, 0)

    def score_line(h, s):
        pl.when(k - s >= 0)(lambda: score(h, 2 * (k - s) + y))
        pl.when((s > 0) & (k + s < line))(lambda: score(h, 2 * (k + s) + y))

    def score_across(h, s):
        def one(kk):
            pl.when(kk != twice(h))(lambda: wait_unit(2 + h, 2 * kk + 1 - y))
            score(h, 2 * kk + 1 - y)

        pl.when(k - s >= 0)(lambda: one(k - s))
        pl.when((s > 0) & (k + s < line))(lambda: one(k + s))

    def core_copy(h, xx):
        return pltpu.make_async_remote_copy(
            src_ref=acc.at[h, 2 * xx + 1 - core],
            dst_ref=crecv.at[h, xx],
            send_sem=csend_sem.at[h, xx],
            recv_sem=crecv_sem.at[h, xx],
            device_id=core_mate,
            device_id_type=MESH,
        )

    def x_copy(h):
        return pltpu.make_async_remote_copy(
            src_ref=xsend.at[h],
            dst_ref=xrecv.at[h],
            send_sem=xsend_sem.at[h],
            recv_sem=xrecv_sem.at[h],
            device_id=x_mate,
            device_id_type=MESH,
        )

    def reduce_open(h):
        core_copy(h, 1 - x).start()
        core_copy(h, x).start()

    def reduce_core(h):
        core_copy(h, 1 - x).wait_recv()
        xsend[h] = (acc[h, 2 * (1 - x) + core] + crecv[h, 1 - x]).astype(jnp.bfloat16)
        x_copy(h).start()

    def reduce_close(h):
        core_copy(h, x).wait_recv()
        x_copy(h).wait_recv()
        total = acc[h, layer] + crecv[h, x] + xrecv[h].astype(jnp.float32)
        out_ref[:, h] = total.reshape(out_ref.shape[0], half_rows, nt)

    open_phase(0)
    load_t.start()
    acc[...] = jnp.zeros_like(acc)
    forward(0, 1)
    forward(0, 2)
    open_phase(1)
    forward_rest(0, 3)
    load_q[0].wait()
    load_p.wait()
    forward(1, 1)
    wait_across(0)
    forward(1, 2)
    condition(0)
    open_phase(2)
    forward_rest(1, 3)
    load_q[1].wait()
    wait_across(1)
    forward(2, 1)
    condition(1)
    forward(2, 2)
    open_phase(3)
    forward_rest(2, 3)
    load_t.wait()

    def first(s, c):
        score_line(0, s - 1)
        forward(3, s)
        return c

    lax.fori_loop(1, line + 1, first, 0)
    lax.fori_loop(0, line, lambda s, c: (score_across(0, s), c)[1], 0)
    reduce_open(0)
    lax.fori_loop(0, line, lambda s, c: (score_line(1, s), c)[1], 0)
    reduce_core(0)

    def last(s, c):
        score_across(1, s)
        pl.when(s == line - 2)(lambda: reduce_close(0))
        return c

    lax.fori_loop(0, line, last, 0)
    reduce_open(1)
    reduce_core(1)
    reduce_close(1)

    for phase in range(4):

        def drain(kk, c):
            pl.when(has_right & (kk <= k))(
                lambda: copy(phase, kk, RIGHT, right).wait_send()
            )
            pl.when(has_left & (kk >= k))(
                lambda: copy(phase, kk, LEFT, left).wait_send()
            )
            pl.when((kk == k) | (kk != twice(phase)))(
                lambda: copy(phase, kk, ACROSS, across).wait_send()
            )
            return c

        lax.fori_loop(0, line, drain, 0)
        pl.when(has_right if phase % 2 == 0 else has_left)(
            lambda: copy(phase, twice(phase), TWICE, across).wait_send()
        )
    for h in range(2):
        core_copy(h, x).wait_send()
        core_copy(h, 1 - x).wait_send()
        x_copy(h).wait_send()


def per_device(units, queries, precond, train_grads):
    own, _, features = queries.shape
    width = precond.shape[2]
    nt = train_grads.shape[0]
    half_rows = own // 2
    nq = units * half_rows
    line = units // 2
    bf16, f32 = jnp.bfloat16, jnp.float32
    anywhere = pl.BlockSpec(memory_space=pl.ANY)
    flops = 2 * 2 * nq * features * (width + nt)
    out = pl.pallas_call(
        functools.partial(kernel, line),
        out_shape=jax.ShapeDtypeStruct((units // 4, 2, half_rows, nt), f32),
        in_specs=[anywhere] * 3,
        out_specs=pl.BlockSpec(memory_space=pltpu.VMEM),
        scratch_shapes=[
            pltpu.VMEM((2, units, half_rows, features), bf16),
            pltpu.VMEM((2, units, nq, width), bf16),
            pltpu.VMEM((features, width), bf16),
            pltpu.VMEM((nt, features), bf16),
            pltpu.VMEM((nq, width), f32),
            pltpu.VMEM((2, 4, nq // 4, nt), f32),
            pltpu.VMEM((2, 2, nq // 4, nt), f32),
            pltpu.VMEM((2, nq // 4, nt), bf16),
            pltpu.VMEM((2, nq // 4, nt), bf16),
            pltpu.SemaphoreType.DMA((4,)),
            pltpu.SemaphoreType.DMA((4, 4, line)),
            pltpu.SemaphoreType.DMA((4, units)),
            pltpu.SemaphoreType.DMA((2, 2)),
            pltpu.SemaphoreType.DMA((2, 2)),
            pltpu.SemaphoreType.DMA((2,)),
            pltpu.SemaphoreType.DMA((2,)),
        ],
        compiler_params=pltpu.CompilerParams(
            collective_id=0, has_side_effects=True, vmem_limit_bytes=60 << 20
        ),
        cost_estimate=pl.CostEstimate(
            flops=flops, bytes_accessed=2 * features * (width + nt), transcendentals=0
        ),
    )(
        queries.reshape(2, half_rows, features),
        precond.reshape(features, width),
        train_grads.reshape(nt, features),
    )
    return out.reshape(2 * units // 4 * half_rows, nt)


def solution(mesh):
    return jax.shard_map(
        functools.partial(per_device, mesh.shape["rows"]),
        mesh=mesh,
        in_specs=(P("rows", "layers", None), P("layers", None, "rows"), P("rows", "layers", None)),
        out_specs=P("layers", "rows"),
        check_vma=False,
    )
```

```python
import functools

import jax
import jax.numpy as jnp
from jax import lax
from jax.experimental import pallas as pl
from jax.experimental.pallas import tpu as pltpu
from jax.sharding import PartitionSpec as P

MESH = pl.DeviceIdType.MESH
RIGHT, LEFT, ACROSS = 0, 1, 2


def kernel(
    line, q_hbm, p_hbm, t_hbm, out_ref,
    qbuf, cbuf, pv, tv, cacc, acc, crecv, xsend, xrecv,
    local_sem, send_sem, recv_sem, csend_sem, crecv_sem, xsend_sem, xrecv_sem,
):
    row, layer = lax.axis_index("rows"), lax.axis_index("layers")
    k, y = row // 2, row % 2
    x, core = layer // 2, layer % 2
    units, half_rows = qbuf.shape[1], qbuf.shape[2]
    width = cbuf.shape[3]
    nq = units * half_rows
    features, nt = tv.shape[1], tv.shape[0]

    def at_row(r):
        return {"rows": r, "layers": layer}

    def at_layer(l):
        return {"rows": row, "layers": l}

    right, left, across = at_row(row + 2), at_row(row - 2), at_row(2 * k + 1 - y)
    has_right, has_left = k + 1 < line, k > 0
    core_mate = at_layer(2 * x + 1 - core)
    x_mate = at_layer(2 * (1 - x) + core)

    load_q = [
        pltpu.make_async_copy(q_hbm.at[h], qbuf.at[h, row], local_sem.at[h])
        for h in range(2)
    ]
    load_p = pltpu.make_async_copy(p_hbm, pv, local_sem.at[2])
    load_t = pltpu.make_async_copy(t_hbm, tv, local_sem.at[3])
    load_q[0].start()
    load_q[1].start()
    load_p.start()

    barrier = pltpu.get_barrier_semaphore()
    for mate in (across, core_mate, x_mate):
        pl.semaphore_signal(barrier, inc=1, device_id=mate, device_id_type=MESH)

    @pl.when(has_right)
    def _():
        pl.semaphore_signal(barrier, inc=1, device_id=right, device_id_type=MESH)

    @pl.when(has_left)
    def _():
        pl.semaphore_signal(barrier, inc=1, device_id=left, device_id_type=MESH)

    neighbours = (k + line - 1) // line + (2 * line - 2 - k) // line
    pl.semaphore_wait(barrier, 3 + neighbours)

    def slot(phase, unit):
        return (qbuf if phase < 2 else cbuf).at[phase % 2, unit]

    def copy(phase, kk, side, target, own=False):
        unit = 2 * kk + y
        return pltpu.make_async_remote_copy(
            src_ref=q_hbm.at[phase] if own and phase < 2 else slot(phase, unit),
            dst_ref=slot(phase, unit),
            send_sem=send_sem.at[phase, side, kk],
            recv_sem=recv_sem.at[phase, unit],
            device_id=target,
            device_id_type=MESH,
        )

    def wait_unit(phase, unit):
        pltpu.make_async_remote_copy(
            src_ref=slot(phase, unit),
            dst_ref=slot(phase, unit),
            send_sem=send_sem.at[phase, ACROSS, 0],
            recv_sem=recv_sem.at[phase, unit],
            device_id=across,
            device_id_type=MESH,
        ).wait_recv()

    def open_phase(phase):
        pl.when(has_right)(lambda: copy(phase, k, RIGHT, right, own=True).start())
        pl.when(has_left)(lambda: copy(phase, k, LEFT, left, own=True).start())
        copy(phase, k, ACROSS, across, own=True).start()

    def forward(phase, s):
        def onward(kk, side, target, more):
            wait_unit(phase, 2 * kk + y)
            pl.when(more)(lambda: copy(phase, kk, side, target).start())
            copy(phase, kk, ACROSS, across).start()

        pl.when(k - s >= 0)(lambda: onward(k - s, RIGHT, right, has_right))
        pl.when(k + s < line)(lambda: onward(k + s, LEFT, left, has_left))

    def wait_across(phase):
        def body(kk, c):
            wait_unit(phase, 2 * kk + 1 - y)
            return c

        lax.fori_loop(0, line, body, 0)

    depth = min(512, features)

    def condition(h):
        cacc[...] = jnp.zeros_like(cacc)

        def body(i, c):
            cut = pl.ds(pl.multiple_of(i * depth, depth), depth)
            cacc[...] += jnp.dot(
                qbuf[h, :, :, cut].reshape(nq, depth), pv[cut, :],
                preferred_element_type=jnp.float32,
            )
            return c

        lax.fori_loop(0, features // depth, body, 0)
        cbuf[h, row] = cacc[...].astype(jnp.bfloat16)

    tile = min(512, nt)

    def score(h, unit):
        cols = pl.ds(pl.multiple_of(unit * width, width), width)

        def body(i, c):
            rows = pl.ds(pl.multiple_of(i * tile, tile), tile)
            part = lax.dot_general(
                cbuf[h, unit], tv[rows, cols], (((1,), (1,)), ((), ())),
                preferred_element_type=jnp.float32,
            )
            acc[h, :, :, rows] += part.reshape(4, nq // 4, tile)
            return c

        lax.fori_loop(0, nt // tile, body, 0)

    def score_line(h, s):
        pl.when(k - s >= 0)(lambda: score(h, 2 * (k - s) + y))
        pl.when((s > 0) & (k + s < line))(lambda: score(h, 2 * (k + s) + y))

    def score_across(h, s):
        def one(kk):
            wait_unit(2 + h, 2 * kk + 1 - y)
            score(h, 2 * kk + 1 - y)

        pl.when(k - s >= 0)(lambda: one(k - s))
        pl.when((s > 0) & (k + s < line))(lambda: one(k + s))

    def core_copy(h, xx):
        return pltpu.make_async_remote_copy(
            src_ref=acc.at[h, 2 * xx + 1 - core],
            dst_ref=crecv.at[h, xx],
            send_sem=csend_sem.at[h, xx],
            recv_sem=crecv_sem.at[h, xx],
            device_id=core_mate,
            device_id_type=MESH,
        )

    def x_copy(h):
        return pltpu.make_async_remote_copy(
            src_ref=xsend.at[h],
            dst_ref=xrecv.at[h],
            send_sem=xsend_sem.at[h],
            recv_sem=xrecv_sem.at[h],
            device_id=x_mate,
            device_id_type=MESH,
        )

    def reduce_open(h):
        core_copy(h, 1 - x).start()
        core_copy(h, x).start()

    def reduce_core(h):
        core_copy(h, 1 - x).wait_recv()
        xsend[h] = (acc[h, 2 * (1 - x) + core] + crecv[h, 1 - x]).astype(jnp.bfloat16)
        x_copy(h).start()

    def reduce_close(h):
        core_copy(h, x).wait_recv()
        x_copy(h).wait_recv()
        total = acc[h, layer] + crecv[h, x] + xrecv[h].astype(jnp.float32)
        out_ref[:, h] = total.reshape(out_ref.shape[0], half_rows, nt)

    open_phase(0)
    open_phase(1)
    load_t.start()
    acc[...] = jnp.zeros_like(acc)

    def gather(s, c):
        forward(0, s)
        forward(1, s)
        return c

    lax.fori_loop(1, line, gather, 0)
    load_q[0].wait()
    load_q[1].wait()
    load_p.wait()
    wait_across(0)
    condition(0)
    open_phase(2)
    wait_across(1)
    condition(1)
    open_phase(3)
    load_t.wait()

    def gather_and_score(s, c):
        forward(2, s)
        forward(3, s)
        score_line(0, s - 1)
        score_line(1, s - 1)
        return c

    lax.fori_loop(1, line, gather_and_score, 0)
    score_line(0, line - 1)
    score_line(1, line - 1)

    def finish(s, c):
        score_across(0, s)
        pl.when(s == line - 1)(lambda: reduce_open(0))
        score_across(1, s)
        return c

    lax.fori_loop(0, line, finish, 0)
    reduce_open(1)
    for h in range(2):
        reduce_core(h)
    for h in range(2):
        reduce_close(h)

    for phase in range(4):

        def drain(kk, c):
            pl.when(has_right & (kk <= k))(
                lambda: copy(phase, kk, RIGHT, right).wait_send()
            )
            pl.when(has_left & (kk >= k))(
                lambda: copy(phase, kk, LEFT, left).wait_send()
            )
            copy(phase, kk, ACROSS, across).wait_send()
            return c

        lax.fori_loop(0, line, drain, 0)
    for h in range(2):
        core_copy(h, x).wait_send()
        core_copy(h, 1 - x).wait_send()
        x_copy(h).wait_send()


def per_device(units, queries, precond, train_grads):
    own, _, features = queries.shape
    width = precond.shape[2]
    nt = train_grads.shape[0]
    half_rows = own // 2
    nq = units * half_rows
    line = units // 2
    bf16, f32 = jnp.bfloat16, jnp.float32
    anywhere = pl.BlockSpec(memory_space=pl.ANY)
    flops = 2 * 2 * nq * features * (width + nt)
    out = pl.pallas_call(
        functools.partial(kernel, line),
        out_shape=jax.ShapeDtypeStruct((units // 4, 2, half_rows, nt), f32),
        in_specs=[anywhere] * 3,
        out_specs=pl.BlockSpec(memory_space=pltpu.VMEM),
        scratch_shapes=[
            pltpu.VMEM((2, units, half_rows, features), bf16),
            pltpu.VMEM((2, units, nq, width), bf16),
            pltpu.VMEM((features, width), bf16),
            pltpu.VMEM((nt, features), bf16),
            pltpu.VMEM((nq, width), f32),
            pltpu.VMEM((2, 4, nq // 4, nt), f32),
            pltpu.VMEM((2, 2, nq // 4, nt), f32),
            pltpu.VMEM((2, nq // 4, nt), bf16),
            pltpu.VMEM((2, nq // 4, nt), bf16),
            pltpu.SemaphoreType.DMA((4,)),
            pltpu.SemaphoreType.DMA((4, 3, line)),
            pltpu.SemaphoreType.DMA((4, units)),
            pltpu.SemaphoreType.DMA((2, 2)),
            pltpu.SemaphoreType.DMA((2, 2)),
            pltpu.SemaphoreType.DMA((2,)),
            pltpu.SemaphoreType.DMA((2,)),
        ],
        compiler_params=pltpu.CompilerParams(
            collective_id=0, has_side_effects=True, vmem_limit_bytes=60 << 20
        ),
        cost_estimate=pl.CostEstimate(
            flops=flops, bytes_accessed=2 * features * (width + nt), transcendentals=0
        ),
    )(
        queries.reshape(2, half_rows, features),
        precond.reshape(features, width),
        train_grads.reshape(nt, features),
    )
    return out.reshape(2 * units // 4 * half_rows, nt)


def solution(mesh):
    return jax.shard_map(
        functools.partial(per_device, mesh.shape["rows"]),
        mesh=mesh,
        in_specs=(P("rows", "layers", None), P("layers", None, "rows"), P("rows", "layers", None)),
        out_specs=P("layers", "rows"),
        check_vma=False,
    )
```

```python
import functools

import jax
import jax.numpy as jnp
from jax import lax
from jax.experimental import pallas as pl
from jax.experimental.pallas import tpu as pltpu
from jax.sharding import PartitionSpec as P

MESH = pl.DeviceIdType.MESH
RIGHT, LEFT, ACROSS = 0, 1, 2


def kernel(
    line, q_hbm, p_hbm, t_hbm, out_ref,
    qbuf, cbuf, pv, tv, cacc, turned, acc, crecv, xsend, xrecv,
    local_sem, send_sem, recv_sem, csend_sem, crecv_sem, xsend_sem, xrecv_sem,
):
    row, layer = lax.axis_index("rows"), lax.axis_index("layers")
    k, y = row // 2, row % 2
    x, core = layer // 2, layer % 2
    units, half_rows = qbuf.shape[1], qbuf.shape[2]
    width = cbuf.shape[3]
    nq = units * half_rows
    features, nt = tv.shape[1], tv.shape[0]

    def at_row(r):
        return {"rows": r, "layers": layer}

    def at_layer(l):
        return {"rows": row, "layers": l}

    right, left, across = at_row(row + 2), at_row(row - 2), at_row(2 * k + 1 - y)
    has_right, has_left = k + 1 < line, k > 0
    core_mate = at_layer(2 * x + 1 - core)
    x_mate = at_layer(2 * (1 - x) + core)

    load_q = [
        pltpu.make_async_copy(q_hbm.at[h], qbuf.at[h, row], local_sem.at[h])
        for h in range(2)
    ]
    load_p = pltpu.make_async_copy(p_hbm, pv, local_sem.at[2])
    load_t = pltpu.make_async_copy(t_hbm, tv, local_sem.at[3])
    load_q[0].start()
    load_q[1].start()
    load_p.start()

    barrier = pltpu.get_barrier_semaphore()
    for mate in (across, core_mate, x_mate):
        pl.semaphore_signal(barrier, inc=1, device_id=mate, device_id_type=MESH)

    @pl.when(has_right)
    def _():
        pl.semaphore_signal(barrier, inc=1, device_id=right, device_id_type=MESH)

    @pl.when(has_left)
    def _():
        pl.semaphore_signal(barrier, inc=1, device_id=left, device_id_type=MESH)

    neighbours = (k + line - 1) // line + (2 * line - 2 - k) // line
    pl.semaphore_wait(barrier, 3 + neighbours)

    def slot(phase, unit):
        return qbuf.at[phase, unit] if phase < 2 else cbuf.at[unit, phase - 2]

    def copy(phase, kk, side, target, own=False):
        unit = 2 * kk + y
        return pltpu.make_async_remote_copy(
            src_ref=q_hbm.at[phase] if own and phase < 2 else slot(phase, unit),
            dst_ref=slot(phase, unit),
            send_sem=send_sem.at[phase, side, kk],
            recv_sem=recv_sem.at[phase, unit],
            device_id=target,
            device_id_type=MESH,
        )

    def wait_unit(phase, unit):
        pltpu.make_async_remote_copy(
            src_ref=slot(phase, unit),
            dst_ref=slot(phase, unit),
            send_sem=send_sem.at[phase, ACROSS, 0],
            recv_sem=recv_sem.at[phase, unit],
            device_id=across,
            device_id_type=MESH,
        ).wait_recv()

    def open_phase(phase):
        pl.when(has_right)(lambda: copy(phase, k, RIGHT, right, own=True).start())
        pl.when(has_left)(lambda: copy(phase, k, LEFT, left, own=True).start())
        copy(phase, k, ACROSS, across, own=True).start()

    def forward(phase, s):
        def onward(kk, side, target, more):
            wait_unit(phase, 2 * kk + y)
            pl.when(more)(lambda: copy(phase, kk, side, target).start())
            copy(phase, kk, ACROSS, across).start()

        pl.when(k - s >= 0)(lambda: onward(k - s, RIGHT, right, has_right))
        pl.when(k + s < line)(lambda: onward(k + s, LEFT, left, has_left))

    def wait_across(phase):
        def body(kk, c):
            wait_unit(phase, 2 * kk + 1 - y)
            return c

        lax.fori_loop(0, line, body, 0)

    depth = min(512, features)

    def condition(h):
        cacc[...] = jnp.zeros_like(cacc)

        def body(i, c):
            cut = pl.ds(pl.multiple_of(i * depth, depth), depth)
            cacc[...] += jnp.dot(
                qbuf[h, :, :, cut].reshape(nq, depth), pv[cut, :],
                preferred_element_type=jnp.float32,
            )
            return c

        lax.fori_loop(0, features // depth, body, 0)
        cbuf[row, h] = cacc[...].astype(jnp.bfloat16)

    tile = min(512, nt)

    def score(unit):
        cols = pl.ds(pl.multiple_of(unit * width, width), width)

        def body(i, c):
            rows = pl.ds(pl.multiple_of(i * tile, tile), tile)
            turned[rows, :] += lax.dot_general(
                tv[rows, cols], cbuf[unit].reshape(2 * nq, width),
                (((1,), (1,)), ((), ())), preferred_element_type=jnp.float32,
            )
            return c

        lax.fori_loop(0, nt // tile, body, 0)

    def score_line(s):
        pl.when(k - s >= 0)(lambda: score(2 * (k - s) + y))
        pl.when((s > 0) & (k + s < line))(lambda: score(2 * (k + s) + y))

    def score_across(s):
        def one(kk):
            wait_unit(2, 2 * kk + 1 - y)
            wait_unit(3, 2 * kk + 1 - y)
            score(2 * kk + 1 - y)

        pl.when(k - s >= 0)(lambda: one(k - s))
        pl.when((s > 0) & (k + s < line))(lambda: one(k + s))

    def turn(h):
        def body(i, c):
            rows = pl.ds(pl.multiple_of(i * tile, tile), tile)
            part = turned[rows, h * nq:(h + 1) * nq].T
            acc[h, :, :, rows] = part.reshape(4, nq // 4, tile)
            return c

        lax.fori_loop(0, nt // tile, body, 0)

    def core_copy(h, xx):
        return pltpu.make_async_remote_copy(
            src_ref=acc.at[h, 2 * xx + 1 - core],
            dst_ref=crecv.at[h, xx],
            send_sem=csend_sem.at[h, xx],
            recv_sem=crecv_sem.at[h, xx],
            device_id=core_mate,
            device_id_type=MESH,
        )

    def x_copy(h):
        return pltpu.make_async_remote_copy(
            src_ref=xsend.at[h],
            dst_ref=xrecv.at[h],
            send_sem=xsend_sem.at[h],
            recv_sem=xrecv_sem.at[h],
            device_id=x_mate,
            device_id_type=MESH,
        )

    def reduce_open(h):
        core_copy(h, 1 - x).start()
        core_copy(h, x).start()

    def reduce_core(h):
        core_copy(h, 1 - x).wait_recv()
        xsend[h] = (acc[h, 2 * (1 - x) + core] + crecv[h, 1 - x]).astype(jnp.bfloat16)
        x_copy(h).start()

    def reduce_close(h):
        core_copy(h, x).wait_recv()
        x_copy(h).wait_recv()
        total = acc[h, layer] + crecv[h, x] + xrecv[h].astype(jnp.float32)
        out_ref[:, h] = total.reshape(out_ref.shape[0], half_rows, nt)

    open_phase(0)
    open_phase(1)
    load_t.start()
    turned[...] = jnp.zeros_like(turned)

    def gather(s, c):
        forward(0, s)
        forward(1, s)
        return c

    lax.fori_loop(1, line, gather, 0)
    load_q[0].wait()
    load_q[1].wait()
    load_p.wait()
    wait_across(0)
    condition(0)
    open_phase(2)
    wait_across(1)
    condition(1)
    open_phase(3)
    load_t.wait()

    def gather_and_score(s, c):
        forward(2, s)
        forward(3, s)
        score_line(s - 1)
        return c

    lax.fori_loop(1, line, gather_and_score, 0)
    score_line(line - 1)

    lax.fori_loop(0, line, lambda s, c: (score_across(s), c)[1], 0)
    for h in range(2):
        turn(h)
        reduce_open(h)
    for h in range(2):
        reduce_core(h)
    for h in range(2):
        reduce_close(h)

    for phase in range(4):

        def drain(kk, c):
            pl.when(has_right & (kk <= k))(
                lambda: copy(phase, kk, RIGHT, right).wait_send()
            )
            pl.when(has_left & (kk >= k))(
                lambda: copy(phase, kk, LEFT, left).wait_send()
            )
            copy(phase, kk, ACROSS, across).wait_send()
            return c

        lax.fori_loop(0, line, drain, 0)
    for h in range(2):
        core_copy(h, x).wait_send()
        core_copy(h, 1 - x).wait_send()
        x_copy(h).wait_send()


def per_device(units, queries, precond, train_grads):
    own, _, features = queries.shape
    width = precond.shape[2]
    nt = train_grads.shape[0]
    half_rows = own // 2
    nq = units * half_rows
    line = units // 2
    bf16, f32 = jnp.bfloat16, jnp.float32
    anywhere = pl.BlockSpec(memory_space=pl.ANY)
    flops = 2 * 2 * nq * features * (width + nt)
    out = pl.pallas_call(
        functools.partial(kernel, line),
        out_shape=jax.ShapeDtypeStruct((units // 4, 2, half_rows, nt), f32),
        in_specs=[anywhere] * 3,
        out_specs=pl.BlockSpec(memory_space=pltpu.VMEM),
        scratch_shapes=[
            pltpu.VMEM((2, units, half_rows, features), bf16),
            pltpu.VMEM((units, 2, nq, width), bf16),
            pltpu.VMEM((features, width), bf16),
            pltpu.VMEM((nt, features), bf16),
            pltpu.VMEM((nq, width), f32),
            pltpu.VMEM((nt, 2 * nq), f32),
            pltpu.VMEM((2, 4, nq // 4, nt), f32),
            pltpu.VMEM((2, 2, nq // 4, nt), f32),
            pltpu.VMEM((2, nq // 4, nt), bf16),
            pltpu.VMEM((2, nq // 4, nt), bf16),
            pltpu.SemaphoreType.DMA((4,)),
            pltpu.SemaphoreType.DMA((4, 3, line)),
            pltpu.SemaphoreType.DMA((4, units)),
            pltpu.SemaphoreType.DMA((2, 2)),
            pltpu.SemaphoreType.DMA((2, 2)),
            pltpu.SemaphoreType.DMA((2,)),
            pltpu.SemaphoreType.DMA((2,)),
        ],
        compiler_params=pltpu.CompilerParams(
            collective_id=0, has_side_effects=True, vmem_limit_bytes=60 << 20
        ),
        cost_estimate=pl.CostEstimate(
            flops=flops, bytes_accessed=2 * features * (width + nt), transcendentals=0
        ),
    )(
        queries.reshape(2, half_rows, features),
        precond.reshape(features, width),
        train_grads.reshape(nt, features),
    )
    return out.reshape(2 * units // 4 * half_rows, nt)


def solution(mesh):
    return jax.shard_map(
        functools.partial(per_device, mesh.shape["rows"]),
        mesh=mesh,
        in_specs=(P("rows", "layers", None), P("layers", None, "rows"), P("rows", "layers", None)),
        out_specs=P("layers", "rows"),
        check_vma=False,
    )
```

```python
import functools

import jax
import jax.numpy as jnp
from jax import lax
from jax.experimental import pallas as pl
from jax.experimental.pallas import tpu as pltpu
from jax.sharding import PartitionSpec as P

MESH = pl.DeviceIdType.MESH
RIGHT, LEFT, ACROSS, TWICE = 0, 1, 2, 3


def kernel(
    line, q_hbm, p_hbm, t_hbm, out_ref,
    qbuf, cbuf, pv, tv, cacc, turned, acc, crecv, xsend, xrecv,
    local_sem, send_sem, recv_sem, csend_sem, crecv_sem, xsend_sem, xrecv_sem,
):
    row, layer = lax.axis_index("rows"), lax.axis_index("layers")
    k, y = row // 2, row % 2
    x, core = layer // 2, layer % 2
    units, half_rows = qbuf.shape[1], qbuf.shape[2]
    width = cbuf.shape[3]
    nq = units * half_rows
    features, nt = tv.shape[1], tv.shape[0]

    def at_row(r):
        return {"rows": r, "layers": layer}

    def at_layer(l):
        return {"rows": row, "layers": l}

    right, left, across = at_row(row + 2), at_row(row - 2), at_row(2 * k + 1 - y)
    has_right, has_left = k + 1 < line, k > 0
    core_mate = at_layer(2 * x + 1 - core)
    x_mate = at_layer(2 * (1 - x) + core)

    load_q = [
        pltpu.make_async_copy(q_hbm.at[h], qbuf.at[h, row], local_sem.at[h])
        for h in range(2)
    ]
    load_p = pltpu.make_async_copy(p_hbm, pv, local_sem.at[2])
    load_t = pltpu.make_async_copy(t_hbm, tv, local_sem.at[3])
    load_q[0].start()
    load_q[1].start()
    load_p.start()

    barrier = pltpu.get_barrier_semaphore()
    for mate in (across, core_mate, x_mate):
        pl.semaphore_signal(barrier, inc=1, device_id=mate, device_id_type=MESH)

    @pl.when(has_right)
    def _():
        pl.semaphore_signal(barrier, inc=1, device_id=right, device_id_type=MESH)

    @pl.when(has_left)
    def _():
        pl.semaphore_signal(barrier, inc=1, device_id=left, device_id_type=MESH)

    neighbours = (k + line - 1) // line + (2 * line - 2 - k) // line
    pl.semaphore_wait(barrier, 3 + neighbours)

    def slot(phase, unit):
        return qbuf.at[phase, unit] if phase < 2 else cbuf.at[unit, phase - 2]

    def copy(phase, kk, side, target, own=False):
        unit = 2 * kk + (1 - y if side == TWICE else y)
        return pltpu.make_async_remote_copy(
            src_ref=q_hbm.at[phase] if own and phase < 2 else slot(phase, unit),
            dst_ref=slot(phase, unit),
            send_sem=send_sem.at[phase, side, kk],
            recv_sem=recv_sem.at[phase, unit],
            device_id=target,
            device_id_type=MESH,
        )

    def twice(phase):
        return 0 if phase % 2 == 0 else line - 1

    def wait_unit(phase, unit):
        pltpu.make_async_remote_copy(
            src_ref=slot(phase, unit),
            dst_ref=slot(phase, unit),
            send_sem=send_sem.at[phase, ACROSS, 0],
            recv_sem=recv_sem.at[phase, unit],
            device_id=across,
            device_id_type=MESH,
        ).wait_recv()

    def open_phase(phase):
        pl.when(has_right)(lambda: copy(phase, k, RIGHT, right, own=True).start())
        pl.when(has_left)(lambda: copy(phase, k, LEFT, left, own=True).start())
        copy(phase, k, ACROSS, across, own=True).start()

    def forward(phase, s):
        def onward(kk, side, target, more):
            wait_unit(phase, 2 * kk + y)
            pl.when(more)(lambda: copy(phase, kk, side, target).start())
            pl.when(kk != twice(phase))(lambda: copy(phase, kk, ACROSS, across).start())

        pl.when(k - s >= 0)(lambda: onward(k - s, RIGHT, right, has_right))
        pl.when(k + s < line)(lambda: onward(k + s, LEFT, left, has_left))
        end = twice(phase)
        distance, side, target, more = (
            (k, RIGHT, right, has_right) if end == 0 else (end - k, LEFT, left, has_left)
        )

        @pl.when(s == distance + 1)
        def _():
            wait_unit(phase, 2 * end + 1 - y)
            pl.when(more)(lambda: copy(phase, end, TWICE, target).start())

    def wait_across(phase):
        def body(kk, c):
            pl.when(kk != twice(phase))(lambda: wait_unit(phase, 2 * kk + 1 - y))
            return c

        lax.fori_loop(0, line, body, 0)

    depth = min(512, features)

    def condition(h):
        cacc[...] = jnp.zeros_like(cacc)

        def body(i, c):
            cut = pl.ds(pl.multiple_of(i * depth, depth), depth)
            cacc[...] += jnp.dot(
                qbuf[h, :, :, cut].reshape(nq, depth), pv[cut, :],
                preferred_element_type=jnp.float32,
            )
            return c

        lax.fori_loop(0, features // depth, body, 0)
        cbuf[row, h] = cacc[...].astype(jnp.bfloat16)

    tile = min(512, nt)

    def score(unit):
        cols = pl.ds(pl.multiple_of(unit * width, width), width)

        def body(i, c):
            rows = pl.ds(pl.multiple_of(i * tile, tile), tile)
            turned[rows, :] += lax.dot_general(
                tv[rows, cols], cbuf[unit].reshape(2 * nq, width),
                (((1,), (1,)), ((), ())), preferred_element_type=jnp.float32,
            )
            return c

        lax.fori_loop(0, nt // tile, body, 0)

    def score_line(s):
        pl.when(k - s >= 0)(lambda: score(2 * (k - s) + y))
        pl.when((s > 0) & (k + s < line))(lambda: score(2 * (k + s) + y))

    def score_across(s):
        def one(kk):
            pl.when(kk != twice(2))(lambda: wait_unit(2, 2 * kk + 1 - y))
            pl.when(kk != twice(3))(lambda: wait_unit(3, 2 * kk + 1 - y))
            score(2 * kk + 1 - y)

        pl.when(k - s >= 0)(lambda: one(k - s))
        pl.when((s > 0) & (k + s < line))(lambda: one(k + s))

    def turn(h):
        def body(i, c):
            rows = pl.ds(pl.multiple_of(i * tile, tile), tile)
            part = turned[rows, h * nq:(h + 1) * nq].T
            acc[h, :, :, rows] = part.reshape(4, nq // 4, tile)
            return c

        lax.fori_loop(0, nt // tile, body, 0)

    def core_copy(h, xx):
        return pltpu.make_async_remote_copy(
            src_ref=acc.at[h, 2 * xx + 1 - core],
            dst_ref=crecv.at[h, xx],
            send_sem=csend_sem.at[h, xx],
            recv_sem=crecv_sem.at[h, xx],
            device_id=core_mate,
            device_id_type=MESH,
        )

    def x_copy(h):
        return pltpu.make_async_remote_copy(
            src_ref=xsend.at[h],
            dst_ref=xrecv.at[h],
            send_sem=xsend_sem.at[h],
            recv_sem=xrecv_sem.at[h],
            device_id=x_mate,
            device_id_type=MESH,
        )

    def reduce_open(h):
        core_copy(h, 1 - x).start()
        core_copy(h, x).start()

    def reduce_core(h):
        core_copy(h, 1 - x).wait_recv()
        xsend[h] = (acc[h, 2 * (1 - x) + core] + crecv[h, 1 - x]).astype(jnp.bfloat16)
        x_copy(h).start()

    def reduce_close(h):
        core_copy(h, x).wait_recv()
        x_copy(h).wait_recv()
        total = acc[h, layer] + crecv[h, x] + xrecv[h].astype(jnp.float32)
        out_ref[:, h] = total.reshape(out_ref.shape[0], half_rows, nt)

    open_phase(0)
    open_phase(1)
    load_t.start()
    turned[...] = jnp.zeros_like(turned)

    def gather(s, c):
        forward(0, s)
        forward(1, s)
        return c

    lax.fori_loop(1, line + 1, gather, 0)
    load_q[0].wait()
    load_q[1].wait()
    load_p.wait()
    wait_across(0)
    condition(0)
    open_phase(2)
    wait_across(1)
    condition(1)
    open_phase(3)
    load_t.wait()

    def gather_and_score(s, c):
        forward(2, s)
        forward(3, s)
        score_line(s - 1)
        return c

    lax.fori_loop(1, line + 1, gather_and_score, 0)

    lax.fori_loop(0, line, lambda s, c: (score_across(s), c)[1], 0)
    for h in range(2):
        turn(h)
        reduce_open(h)
    for h in range(2):
        reduce_core(h)
    for h in range(2):
        reduce_close(h)

    for phase in range(4):

        def drain(kk, c):
            pl.when(has_right & (kk <= k))(
                lambda: copy(phase, kk, RIGHT, right).wait_send()
            )
            pl.when(has_left & (kk >= k))(
                lambda: copy(phase, kk, LEFT, left).wait_send()
            )
            pl.when((kk == k) | (kk != twice(phase)))(
                lambda: copy(phase, kk, ACROSS, across).wait_send()
            )
            return c

        lax.fori_loop(0, line, drain, 0)
        pl.when(has_right if phase % 2 == 0 else has_left)(
            lambda: copy(phase, twice(phase), TWICE, across).wait_send()
        )
    for h in range(2):
        core_copy(h, x).wait_send()
        core_copy(h, 1 - x).wait_send()
        x_copy(h).wait_send()


def per_device(units, queries, precond, train_grads):
    own, _, features = queries.shape
    width = precond.shape[2]
    nt = train_grads.shape[0]
    half_rows = own // 2
    nq = units * half_rows
    line = units // 2
    bf16, f32 = jnp.bfloat16, jnp.float32
    anywhere = pl.BlockSpec(memory_space=pl.ANY)
    flops = 2 * 2 * nq * features * (width + nt)
    out = pl.pallas_call(
        functools.partial(kernel, line),
        out_shape=jax.ShapeDtypeStruct((units // 4, 2, half_rows, nt), f32),
        in_specs=[anywhere] * 3,
        out_specs=pl.BlockSpec(memory_space=pltpu.VMEM),
        scratch_shapes=[
            pltpu.VMEM((2, units, half_rows, features), bf16),
            pltpu.VMEM((units, 2, nq, width), bf16),
            pltpu.VMEM((features, width), bf16),
            pltpu.VMEM((nt, features), bf16),
            pltpu.VMEM((nq, width), f32),
            pltpu.VMEM((nt, 2 * nq), f32),
            pltpu.VMEM((2, 4, nq // 4, nt), f32),
            pltpu.VMEM((2, 2, nq // 4, nt), f32),
            pltpu.VMEM((2, nq // 4, nt), bf16),
            pltpu.VMEM((2, nq // 4, nt), bf16),
            pltpu.SemaphoreType.DMA((4,)),
            pltpu.SemaphoreType.DMA((4, 4, line)),
            pltpu.SemaphoreType.DMA((4, units)),
            pltpu.SemaphoreType.DMA((2, 2)),
            pltpu.SemaphoreType.DMA((2, 2)),
            pltpu.SemaphoreType.DMA((2,)),
            pltpu.SemaphoreType.DMA((2,)),
        ],
        compiler_params=pltpu.CompilerParams(
            collective_id=0, has_side_effects=True, vmem_limit_bytes=60 << 20
        ),
        cost_estimate=pl.CostEstimate(
            flops=flops, bytes_accessed=2 * features * (width + nt), transcendentals=0
        ),
    )(
        queries.reshape(2, half_rows, features),
        precond.reshape(features, width),
        train_grads.reshape(nt, features),
    )
    return out.reshape(2 * units // 4 * half_rows, nt)


def solution(mesh):
    return jax.shard_map(
        functools.partial(per_device, mesh.shape["rows"]),
        mesh=mesh,
        in_specs=(P("rows", "layers", None), P("layers", None, "rows"), P("rows", "layers", None)),
        out_specs=P("layers", "rows"),
        check_vma=False,
    )
```

```python
import functools

import jax
import jax.numpy as jnp
from jax import lax
from jax.experimental import pallas as pl
from jax.experimental.pallas import tpu as pltpu
from jax.sharding import PartitionSpec as P

MESH = pl.DeviceIdType.MESH
RIGHT, LEFT, ACROSS = 0, 1, 2


def kernel(
    line, q_hbm, p_hbm, t_hbm, out_ref,
    qbuf, cbuf, pv, tv, cacc, turned, acc, crecv, xsend, xrecv,
    local_sem, send_sem, recv_sem, csend_sem, crecv_sem, xsend_sem, xrecv_sem,
):
    row, layer = lax.axis_index("rows"), lax.axis_index("layers")
    k, y = row // 2, row % 2
    x, core = layer // 2, layer % 2
    units, half_rows = qbuf.shape[1], qbuf.shape[2]
    width = cbuf.shape[3]
    nq = units * half_rows
    features, nt = tv.shape[1], tv.shape[0]

    def at_row(r):
        return {"rows": r, "layers": layer}

    def at_layer(l):
        return {"rows": row, "layers": l}

    right, left, across = at_row(row + 2), at_row(row - 2), at_row(2 * k + 1 - y)
    has_right, has_left = k + 1 < line, k > 0
    core_mate = at_layer(2 * x + 1 - core)
    x_mate = at_layer(2 * (1 - x) + core)

    load_q = [
        pltpu.make_async_copy(q_hbm.at[h], qbuf.at[h, row], local_sem.at[h])
        for h in range(2)
    ]
    load_p = pltpu.make_async_copy(p_hbm, pv, local_sem.at[2])
    load_t = pltpu.make_async_copy(t_hbm, tv, local_sem.at[3])
    load_q[0].start()
    load_q[1].start()
    load_p.start()

    barrier = pltpu.get_barrier_semaphore()
    for mate in (across, core_mate, x_mate):
        pl.semaphore_signal(barrier, inc=1, device_id=mate, device_id_type=MESH)

    @pl.when(has_right)
    def _():
        pl.semaphore_signal(barrier, inc=1, device_id=right, device_id_type=MESH)

    @pl.when(has_left)
    def _():
        pl.semaphore_signal(barrier, inc=1, device_id=left, device_id_type=MESH)

    neighbours = (k + line - 1) // line + (2 * line - 2 - k) // line
    pl.semaphore_wait(barrier, 3 + neighbours)

    def slot(phase, unit):
        return qbuf.at[phase, unit] if phase < 2 else cbuf.at[unit, phase - 2]

    def copy(phase, kk, side, target, own=False):
        unit = 2 * kk + y
        return pltpu.make_async_remote_copy(
            src_ref=q_hbm.at[phase] if own and phase < 2 else slot(phase, unit),
            dst_ref=slot(phase, unit),
            send_sem=send_sem.at[phase, side, kk],
            recv_sem=recv_sem.at[phase, unit],
            device_id=target,
            device_id_type=MESH,
        )

    def wait_unit(phase, unit):
        pltpu.make_async_remote_copy(
            src_ref=slot(phase, unit),
            dst_ref=slot(phase, unit),
            send_sem=send_sem.at[phase, ACROSS, 0],
            recv_sem=recv_sem.at[phase, unit],
            device_id=across,
            device_id_type=MESH,
        ).wait_recv()

    def open_phase(phase):
        pl.when(has_right)(lambda: copy(phase, k, RIGHT, right, own=True).start())
        pl.when(has_left)(lambda: copy(phase, k, LEFT, left, own=True).start())
        copy(phase, k, ACROSS, across, own=True).start()

    def forward(phase, s):
        def onward(kk, side, target, more):
            wait_unit(phase, 2 * kk + y)
            pl.when(more)(lambda: copy(phase, kk, side, target).start())
            copy(phase, kk, ACROSS, across).start()

        pl.when(k - s >= 0)(lambda: onward(k - s, RIGHT, right, has_right))
        pl.when(k + s < line)(lambda: onward(k + s, LEFT, left, has_left))

    def wait_across(phase):
        def body(kk, c):
            wait_unit(phase, 2 * kk + 1 - y)
            return c

        lax.fori_loop(0, line, body, 0)

    depth = min(2048, features)

    def condition(h):
        cacc[...] = jnp.zeros_like(cacc)

        def body(i, c):
            cut = pl.ds(pl.multiple_of(i * depth, depth), depth)
            cacc[...] += jnp.dot(
                qbuf[h, :, :, cut].reshape(nq, depth), pv[cut, :],
                preferred_element_type=jnp.float32,
            )
            return c

        lax.fori_loop(0, features // depth, body, 0)
        cbuf[row, h] = cacc[...].astype(jnp.bfloat16)

    tile = min(512, nt)

    def score(unit):
        cols = pl.ds(pl.multiple_of(unit * width, width), width)

        def body(i, c):
            rows = pl.ds(pl.multiple_of(i * tile, tile), tile)
            turned[rows, :] += lax.dot_general(
                tv[rows, cols], cbuf[unit].reshape(2 * nq, width),
                (((1,), (1,)), ((), ())), preferred_element_type=jnp.float32,
            )
            return c

        lax.fori_loop(0, nt // tile, body, 0)

    def score_line(s):
        pl.when(k - s >= 0)(lambda: score(2 * (k - s) + y))
        pl.when((s > 0) & (k + s < line))(lambda: score(2 * (k + s) + y))

    def score_across(s):
        def one(kk):
            wait_unit(2, 2 * kk + 1 - y)
            wait_unit(3, 2 * kk + 1 - y)
            score(2 * kk + 1 - y)

        pl.when(k - s >= 0)(lambda: one(k - s))
        pl.when((s > 0) & (k + s < line))(lambda: one(k + s))

    def turn(h):
        def body(i, c):
            rows = pl.ds(pl.multiple_of(i * tile, tile), tile)
            part = turned[rows, h * nq:(h + 1) * nq].T
            acc[h, :, :, rows] = part.reshape(4, nq // 4, tile)
            return c

        lax.fori_loop(0, nt // tile, body, 0)

    def core_copy(h, xx):
        return pltpu.make_async_remote_copy(
            src_ref=acc.at[h, 2 * xx + 1 - core],
            dst_ref=crecv.at[h, xx],
            send_sem=csend_sem.at[h, xx],
            recv_sem=crecv_sem.at[h, xx],
            device_id=core_mate,
            device_id_type=MESH,
        )

    def x_copy(h):
        return pltpu.make_async_remote_copy(
            src_ref=xsend.at[h],
            dst_ref=xrecv.at[h],
            send_sem=xsend_sem.at[h],
            recv_sem=xrecv_sem.at[h],
            device_id=x_mate,
            device_id_type=MESH,
        )

    def reduce_open(h):
        core_copy(h, 1 - x).start()
        core_copy(h, x).start()

    def reduce_core(h):
        core_copy(h, 1 - x).wait_recv()
        xsend[h] = (acc[h, 2 * (1 - x) + core] + crecv[h, 1 - x]).astype(jnp.bfloat16)
        x_copy(h).start()

    def reduce_close(h):
        core_copy(h, x).wait_recv()
        x_copy(h).wait_recv()
        total = acc[h, layer] + crecv[h, x] + xrecv[h].astype(jnp.float32)
        out_ref[:, h] = total.reshape(out_ref.shape[0], half_rows, nt)

    open_phase(0)
    open_phase(1)
    load_t.start()
    turned[...] = jnp.zeros_like(turned)

    def gather(s, c):
        forward(0, s)
        forward(1, s)
        return c

    lax.fori_loop(1, line, gather, 0)
    load_q[0].wait()
    load_q[1].wait()
    load_p.wait()
    wait_across(0)
    condition(0)
    open_phase(2)
    wait_across(1)
    condition(1)
    open_phase(3)
    load_t.wait()

    def gather_and_score(s, c):
        forward(2, s)
        forward(3, s)
        score_line(s - 1)
        return c

    lax.fori_loop(1, line, gather_and_score, 0)
    score_line(line - 1)

    lax.fori_loop(0, line, lambda s, c: (score_across(s), c)[1], 0)
    for h in range(2):
        turn(h)
        reduce_open(h)
    for h in range(2):
        reduce_core(h)
    for h in range(2):
        reduce_close(h)

    for phase in range(4):

        def drain(kk, c):
            pl.when(has_right & (kk <= k))(
                lambda: copy(phase, kk, RIGHT, right).wait_send()
            )
            pl.when(has_left & (kk >= k))(
                lambda: copy(phase, kk, LEFT, left).wait_send()
            )
            copy(phase, kk, ACROSS, across).wait_send()
            return c

        lax.fori_loop(0, line, drain, 0)
    for h in range(2):
        core_copy(h, x).wait_send()
        core_copy(h, 1 - x).wait_send()
        x_copy(h).wait_send()


def per_device(units, queries, precond, train_grads):
    own, _, features = queries.shape
    width = precond.shape[2]
    nt = train_grads.shape[0]
    half_rows = own // 2
    nq = units * half_rows
    line = units // 2
    bf16, f32 = jnp.bfloat16, jnp.float32
    anywhere = pl.BlockSpec(memory_space=pl.ANY)
    flops = 2 * 2 * nq * features * (width + nt)
    out = pl.pallas_call(
        functools.partial(kernel, line),
        out_shape=jax.ShapeDtypeStruct((units // 4, 2, half_rows, nt), f32),
        in_specs=[anywhere] * 3,
        out_specs=pl.BlockSpec(memory_space=pltpu.VMEM),
        scratch_shapes=[
            pltpu.VMEM((2, units, half_rows, features), bf16),
            pltpu.VMEM((units, 2, nq, width), bf16),
            pltpu.VMEM((features, width), bf16),
            pltpu.VMEM((nt, features), bf16),
            pltpu.VMEM((nq, width), f32),
            pltpu.VMEM((nt, 2 * nq), f32),
            pltpu.VMEM((2, 4, nq // 4, nt), f32),
            pltpu.VMEM((2, 2, nq // 4, nt), f32),
            pltpu.VMEM((2, nq // 4, nt), bf16),
            pltpu.VMEM((2, nq // 4, nt), bf16),
            pltpu.SemaphoreType.DMA((4,)),
            pltpu.SemaphoreType.DMA((4, 3, line)),
            pltpu.SemaphoreType.DMA((4, units)),
            pltpu.SemaphoreType.DMA((2, 2)),
            pltpu.SemaphoreType.DMA((2, 2)),
            pltpu.SemaphoreType.DMA((2,)),
            pltpu.SemaphoreType.DMA((2,)),
        ],
        compiler_params=pltpu.CompilerParams(
            collective_id=0, has_side_effects=True, vmem_limit_bytes=60 << 20
        ),
        cost_estimate=pl.CostEstimate(
            flops=flops, bytes_accessed=2 * features * (width + nt), transcendentals=0
        ),
    )(
        queries.reshape(2, half_rows, features),
        precond.reshape(features, width),
        train_grads.reshape(nt, features),
    )
    return out.reshape(2 * units // 4 * half_rows, nt)


def solution(mesh):
    return jax.shard_map(
        functools.partial(per_device, mesh.shape["rows"]),
        mesh=mesh,
        in_specs=(P("rows", "layers", None), P("layers", None, "rows"), P("rows", "layers", None)),
        out_specs=P("layers", "rows"),
        check_vma=False,
    )
```
